32 devices in a mesh: groups: 2 (over x), section: 16 (over z, y, core).
Axes of the slice: x: 2, y: 2, z: 4, core: 2. Of those that a mesh axis runs over, the one named last changes fastest.
Arguments:
- latent_rows: bfloat16 [32, 256, 1408], P(('groups', 'section')), parts along dimension 0, may hold values from -6 to 6
- skip_queue: bfloat16 [32, 256, 1408], P(('groups', 'section')), parts along dimension 0, may hold values from -6 to 6
- norm_gain: float32 [16, 1408], P('section'), may hold values from 0.1 to 1.9
- skip_weight: bfloat16 [16, 2816, 1408], P('section'), may hold values from -0.109375 to 0.109375
- up_weight: bfloat16 [16, 1408, 3072], P('section'), may hold values from -0.15625 to 0.15625
- down_weight: bfloat16 [16, 3072, 1408], P('section'), may hold values from -0.109375 to 0.109375
Outputs:
- next_rows: bfloat16 [32, 256, 1408], P(('groups', 'section')), parts along dimension 0
- next_queue: bfloat16 [32, 256, 1408], P(('groups', 'section')), parts along dimension 0
The draws below stay inside these ranges and needn't reach their ends.
There are 2 independent parts, one for each index of `groups`. The reference program is written for one: setup_inputs(seed, part) draws one part's arguments, and reference() takes and returns one part's arrays. A program takes and returns all parts, laid end to end along the dimension named above; an argument that names none is the same for every part. Nothing has to cross between parts.
All inputs are finite; a program needn't handle non-finite values.
Results may differ from the reference program's by a relative error of at most 0.008.
Values may be sent and summed in bfloat16 or wider, within the bound.
No kernel may reach another device: no remote copies, remote signals or barrier semaphores. Data moves between devices by JAX's collectives and lax.ppermute only.
A program may use at most 128 MiB of HBM per device.

```python
import jax
import jax.numpy as jnp
from jax import lax

D = 1408
FFW = 3072
TICKS = 3
SECTIONS = 16
ROWS = 256


def steps_of(stream_key, extent, pieces, low, largest):
    level = 1.0
    for position, shards_of in pieces:
        heights = jax.random.uniform(jax.random.fold_in(jax.random.fold_in(stream_key, 6), position), (shards_of,), jnp.float32, low / len(pieces), largest / len(pieces))
        level = level * jnp.repeat(jnp.exp(heights), extent[position] // shards_of).reshape((-1,) + (1,) * (len(extent) - 1 - position))
    return level


def scatter_about(rng, dims, width, bound, cuts=(), held_as=jnp.bfloat16):
    entries = width * jax.random.normal(rng, dims, jnp.float32)
    if cuts:
        entries = entries * steps_of(rng, dims, cuts, -0.22, 0.18)
    return jnp.clip(entries, -bound, bound).astype(held_as)


def setup_inputs(seed: int = 0, part: int = 0) -> dict:
    arg_keys = jax.random.split(jax.random.key(seed), 7)
    part_splits = jax.random.split(jax.random.fold_in(arg_keys[6], part), 7)
    return {
        "latent_rows": scatter_about(part_splits[0], (SECTIONS, ROWS, D), 1.0, 6.0, ((0, 16),)),
        "skip_queue": scatter_about(part_splits[1], (SECTIONS, ROWS, D), 1.0, 6.0, ((0, 16),)),
        "norm_gain": jnp.clip(1.0 + 0.18 * jax.random.normal(arg_keys[2], (SECTIONS, D), jnp.float32), 0.1, 1.9),
        "skip_weight": scatter_about(arg_keys[3], (SECTIONS, 2 * D, D), (2 * D) ** -0.5, 0.109375, ((0, 16),)),
        "up_weight": scatter_about(arg_keys[4], (SECTIONS, D, FFW), D ** -0.5, 0.15625, ((0, 16),)),
        "down_weight": scatter_about(arg_keys[5], (SECTIONS, FFW, D), FFW ** -0.5, 0.109375, ((0, 16),)),
    }


epsilon = 1e-06

def block(items):
    current, queue_row, decoder, gain, merging, upper, lower = items
    joined = jnp.concatenate([current, queue_row], axis=1)
    mixed = jnp.dot(joined, merging, preferred_element_type=jnp.float32)
    merged = jnp.where(decoder, mixed, current.astype(jnp.float32))
    center = lax.optimization_barrier(jnp.mean(merged, axis=1, keepdims=True))
    spread = lax.optimization_barrier(jnp.mean(jnp.square(merged - center), axis=1, keepdims=True))
    normed = ((merged - center) * lax.rsqrt(spread + epsilon) * gain).astype(jnp.bfloat16)
    hidden = jax.nn.gelu(jnp.dot(normed, upper, preferred_element_type=jnp.float32), approximate=True).astype(jnp.bfloat16)
    return (merged + jnp.dot(hidden, lower, preferred_element_type=jnp.float32)).astype(jnp.bfloat16)

def reference(latent_rows, skip_queue, norm_gain, skip_weight, up_weight, down_weight):
    sections = latent_rows.shape[0]
    halfway = sections // 2
    decoder_flags = jnp.arange(sections) >= halfway
    current = latent_rows
    queue_now = skip_queue
    for repeat in range(TICKS):
        output = lax.map(block, (current, queue_now, decoder_flags, norm_gain, skip_weight, up_weight, down_weight))
        current = jnp.concatenate([output[-1:], output[:-1]], axis=0)
        queue_now = jnp.concatenate([output[:halfway], queue_now[:halfway][::-1]], axis=0)
    return (current, queue_now)
```

```python
import jax
import jax.numpy as jnp
from jax import lax
from jax.sharding import PartitionSpec as P

TICKS = 3


epsilon = 1e-06


def from_behind(value, axis, steps):
    count = lax.axis_size(axis)
    pairs = [(source, (source + steps) % count) for source in range(count)]
    return lax.ppermute(value, axis, pairs)


def to_mirror(value, axis):
    count = lax.axis_size(axis)
    pairs = [(source, count - 1 - source) for source in range(count // 2)]
    return lax.ppermute(value, axis, pairs)


def local(latent_rows, skip_queue, norm_gain, skip_weight, up_weight, down_weight):
    sections = lax.axis_size("section")
    halfway = sections // 2
    position = lax.axis_index("section")
    decoder = position >= halfway
    current = latent_rows[0]
    queue_now = skip_queue[0]
    gain = norm_gain[0]
    merging = skip_weight[0]
    upper = up_weight[0]
    lower = down_weight[0]
    for repeat in range(TICKS):
        incoming = current
        compute_waiting = queue_now

        def with_skip():
            joined = jnp.concatenate([incoming, compute_waiting], axis=1)
            return jnp.dot(joined, merging, preferred_element_type=jnp.float32)

        def without_skip():
            return incoming.astype(jnp.float32)

        arrived = to_mirror(queue_now, "section")
        merged = lax.cond(decoder, with_skip, without_skip)
        center = jnp.mean(merged, axis=1, keepdims=True)
        spread = jnp.mean(jnp.square(merged - center), axis=1, keepdims=True)
        normed = ((merged - center) * lax.rsqrt(spread + epsilon) * gain).astype(jnp.bfloat16)
        hidden = jax.nn.gelu(
            jnp.dot(normed, upper, preferred_element_type=jnp.float32), approximate=True
        ).astype(jnp.bfloat16)
        output = (merged + jnp.dot(hidden, lower, preferred_element_type=jnp.float32)).astype(
            jnp.bfloat16
        )
        current = from_behind(output, "section", 1)
        queue_now = jnp.where(decoder, arrived, output)
    return (current[None], queue_now[None])


def solution(mesh):
    return jax.shard_map(
        local,
        mesh=mesh,
        in_specs=(
            P(("groups", "section"), None, None),
            P(("groups", "section"), None, None),
            P("section", None),
            P("section", None, None),
            P("section", None, None),
            P("section", None, None),
        ),
        out_specs=(P(("groups", "section"), None, None), P(("groups", "section"), None, None)),
        check_vma=False,
    )
```

```python
import functools

import jax
import jax.numpy as jnp
from jax import lax
from jax.experimental import pallas as pl
from jax.experimental.pallas import tpu as pltpu
from jax.sharding import PartitionSpec as P

TICKS = 3


epsilon = 1e-06


def from_behind(value, axis, steps):
    count = lax.axis_size(axis)
    pairs = [(source, (source + steps) % count) for source in range(count)]
    return lax.ppermute(value, axis, pairs)


def to_mirror(value, axis):
    count = lax.axis_size(axis)
    pairs = [(source, count - 1 - source) for source in range(count // 2)]
    return lax.ppermute(value, axis, pairs)


def spans(extent, step):
    return [(start, min(step, extent - start)) for start in range(0, extent, step)]


def tick_kernel(
    rows_hbm, queue_hbm, gain_ref, merging_hbm, upper_hbm, lower_hbm, out_ref,
    rows, queue, merging, upper, lower, merged, total, row_sem, merging_sem, upper_sem, lower_sem,
    *, step,
):
    decoder = lax.axis_index("section") >= lax.axis_size("section") // 2
    width = rows.shape[1]
    merge_spans = [
        (base + start, size) for base in (0, width) for start, size in spans(width, step)
    ]
    hidden_spans = spans(upper.shape[1], step)

    rows_copy = pltpu.make_async_copy(rows_hbm, rows, row_sem.at[0])
    queue_copy = pltpu.make_async_copy(queue_hbm, queue, row_sem.at[1])
    merging_copies = [
        pltpu.make_async_copy(
            merging_hbm.at[pl.ds(start, size), :], merging.at[pl.ds(start, size), :], merging_sem.at[i]
        )
        for i, (start, size) in enumerate(merge_spans)
    ]
    upper_copies = [
        pltpu.make_async_copy(
            upper_hbm.at[:, pl.ds(start, size)], upper.at[:, pl.ds(start, size)], upper_sem.at[i]
        )
        for i, (start, size) in enumerate(hidden_spans)
    ]
    lower_copies = [
        pltpu.make_async_copy(
            lower_hbm.at[pl.ds(start, size), :], lower.at[pl.ds(start, size), :], lower_sem.at[i]
        )
        for i, (start, size) in enumerate(hidden_spans)
    ]

    rows_copy.start()

    @pl.when(decoder)
    def _():
        queue_copy.start()
        for copy in merging_copies:
            copy.start()

    for first, second in zip(upper_copies, lower_copies):
        first.start()
        second.start()

    rows_copy.wait()

    @pl.when(decoder)
    def _():
        queue_copy.wait()
        value = None
        for (start, size), copy in zip(merge_spans, merging_copies):
            copy.wait()
            source = rows if start < width else queue
            part = jnp.dot(
                source[:, pl.ds(start % width, size)], merging[pl.ds(start, size), :],
                preferred_element_type=jnp.float32,
            )
            value = part if value is None else value + part
        merged[...] = value

    @pl.when(jnp.logical_not(decoder))
    def _():
        merged[...] = rows[...].astype(jnp.float32)

    value = merged[...]
    center = jnp.mean(value, axis=1, keepdims=True)
    spread = jnp.mean(jnp.square(value - center), axis=1, keepdims=True)
    normed = ((value - center) * lax.rsqrt(spread + epsilon) * gain_ref[...]).astype(jnp.bfloat16)
    for i, (start, size) in enumerate(hidden_spans):
        upper_copies[i].wait()
        raised = jnp.dot(normed, upper[:, pl.ds(start, size)], preferred_element_type=jnp.float32)
        hidden = jax.nn.gelu(raised, approximate=True).astype(jnp.bfloat16)
        lower_copies[i].wait()
        part = jnp.dot(hidden, lower[pl.ds(start, size), :], preferred_element_type=jnp.float32)
        if i == 0:
            total[...] = merged[...] + part
        elif i < len(hidden_spans) - 1:
            total[...] += part
        else:
            out_ref[...] = (total[...] + part).astype(out_ref.dtype)


def tick(rows, queue, gain, merging, upper, lower):
    row_count, width = rows.shape
    hidden = upper.shape[1]
    step = 512
    merge_count = 2 * len(spans(width, step))
    hidden_count = len(spans(hidden, step))
    anywhere = pl.BlockSpec(memory_space=pl.ANY)
    flops = 2 * row_count * width * (2 * width + 2 * hidden)
    moved = 2 * (2 * width * width + 2 * width * hidden + 3 * row_count * width)
    return pl.pallas_call(
        functools.partial(tick_kernel, step=step),
        out_shape=jax.ShapeDtypeStruct((row_count, width), jnp.bfloat16),
        in_specs=[anywhere, anywhere, pl.BlockSpec(memory_space=pltpu.VMEM), anywhere, anywhere, anywhere],
        out_specs=pl.BlockSpec(memory_space=pltpu.VMEM),
        scratch_shapes=[
            pltpu.VMEM((row_count, width), jnp.bfloat16),
            pltpu.VMEM((row_count, width), jnp.bfloat16),
            pltpu.VMEM(merging.shape, jnp.bfloat16),
            pltpu.VMEM(upper.shape, jnp.bfloat16),
            pltpu.VMEM(lower.shape, jnp.bfloat16),
            pltpu.VMEM((row_count, width), jnp.float32),
            pltpu.VMEM((row_count, width), jnp.float32),
            pltpu.SemaphoreType.DMA((2,)),
            pltpu.SemaphoreType.DMA((merge_count,)),
            pltpu.SemaphoreType.DMA((hidden_count,)),
            pltpu.SemaphoreType.DMA((hidden_count,)),
        ],
        compiler_params=pltpu.CompilerParams(vmem_limit_bytes=48 * 1024 * 1024),
        cost_estimate=pl.CostEstimate(
            flops=flops, bytes_accessed=moved, transcendentals=row_count * hidden
        ),
        name="tick",
    )(rows, queue, gain, merging, upper, lower)


def local(latent_rows, skip_queue, norm_gain, skip_weight, up_weight, down_weight):
    sections = lax.axis_size("section")
    decoder = lax.axis_index("section") >= sections // 2
    current = latent_rows[0]
    waiting = skip_queue[0]
    sent = waiting
    for repeat in range(TICKS):
        arrived = to_mirror(sent, "section")
        output = tick(current, waiting, norm_gain, skip_weight[0], up_weight[0], down_weight[0])
        current = from_behind(output, "section", 1)
        waiting = arrived
        sent = output
    queue_now = jnp.where(decoder, arrived, output)
    return (current[None], queue_now[None])


def solution(mesh):
    return jax.shard_map(
        local,
        mesh=mesh,
        in_specs=(
            P(("groups", "section"), None, None),
            P(("groups", "section"), None, None),
            P("section", None),
            P("section", None, None),
            P("section", None, None),
            P("section", None, None),
        ),
        out_specs=(P(("groups", "section"), None, None), P(("groups", "section"), None, None)),
        check_vma=False,
    )
```

```python
import functools

import jax
import jax.numpy as jnp
from jax import lax
from jax.experimental import pallas as pl
from jax.experimental.pallas import tpu as pltpu
from jax.sharding import PartitionSpec as P

TICKS = 3


epsilon = 1e-06


def move(value, pairs):
    return lax.ppermute(value, "section", pairs)


def spans(extent, step):
    cuts = [0] + list(range(min(step // 2, extent), extent, step)) + [extent]
    return [(start, stop - start) for start, stop in zip(cuts[:-1], cuts[1:])]


def even_spans(extent, step):
    return [(start, min(step, extent - start)) for start in range(0, extent, step)]


def block_kernel(
    *refs, row_sources, queue_sources, role, step, merge_step,
):
    rows_hbm, refs = refs[: len(row_sources)], refs[len(row_sources) :]
    queue_hbm, refs = refs[: len(queue_sources)], refs[len(queue_sources) :]
    (
        gain_ref, merging_hbm, upper_hbm, lower_hbm, after_hbm, out_ref,
        rows, queue, merging, upper, lower, merged, total, row_sem, merging_sem, upper_sem, lower_sem,
    ) = refs
    section = lax.axis_index("section")
    decoder = section >= lax.axis_size("section") // 2
    width = rows.shape[1]
    merge_spans = [(base + start, size) for base in (0, width) for start, size in even_spans(width, merge_step)]
    hidden_spans = spans(upper.shape[1], step)

    row_copies = [pltpu.make_async_copy(source, rows, row_sem.at[0]) for source in rows_hbm]
    queue_copies = [pltpu.make_async_copy(source, queue, row_sem.at[1]) for source in queue_hbm]
    merging_copies = [
        pltpu.make_async_copy(
            merging_hbm.at[pl.ds(start, size), :], merging.at[pl.ds(start, size), :], merging_sem.at[i]
        )
        for i, (start, size) in enumerate(merge_spans)
    ]
    upper_copies = [
        pltpu.make_async_copy(
            upper_hbm.at[:, pl.ds(start, size)], upper.at[:, pl.ds(start, size)], upper_sem.at[i]
        )
        for i, (start, size) in enumerate(hidden_spans)
    ]
    lower_copies = [
        pltpu.make_async_copy(
            lower_hbm.at[pl.ds(start, size), :], lower.at[pl.ds(start, size), :], lower_sem.at[i]
        )
        for i, (start, size) in enumerate(hidden_spans)
    ]

    def start_one(tests, copies):
        for test, copy in zip(tests, copies):
            if test is None:
                copy.start()
            else:
                pl.when(test(section))(copy.start)

    def work():
        start_one(row_sources, row_copies)

        @pl.when(decoder)
        def _():
            if not queue_copies:
                return
            start_one(queue_sources, queue_copies)
            for copy in merging_copies:
                copy.start()

        for first, second in zip(upper_copies, lower_copies):
            first.start()
            second.start()

        row_copies[0].wait()

        @pl.when(decoder)
        def _():
            if not queue_copies:
                return
            queue_copies[0].wait()
            value = None
            for (start, size), copy in zip(merge_spans, merging_copies):
                copy.wait()
                source = rows if start < width else queue
                part = jnp.dot(
                    source[:, pl.ds(start % width, size)], merging[pl.ds(start, size), :],
                    preferred_element_type=jnp.float32,
                )
                value = part if value is None else value + part
            merged[...] = value

        @pl.when(jnp.logical_not(decoder))
        def _():
            merged[...] = rows[...].astype(jnp.float32)

        value = merged[...]
        center = jnp.mean(value, axis=1, keepdims=True)
        spread = jnp.mean(jnp.square(value - center), axis=1, keepdims=True)
        normed = ((value - center) * lax.rsqrt(spread + epsilon) * gain_ref[...]).astype(jnp.bfloat16)
        for i, (start, size) in enumerate(hidden_spans):
            upper_copies[i].wait()
            raised = jnp.dot(normed, upper[:, pl.ds(start, size)], preferred_element_type=jnp.float32)
            hidden = jax.nn.gelu(raised, approximate=True).astype(jnp.bfloat16)
            lower_copies[i].wait()
            part = jnp.dot(hidden, lower[pl.ds(start, size), :], preferred_element_type=jnp.float32)
            if i == 0:
                total[...] = merged[...] + part
            elif i < len(hidden_spans) - 1:
                total[...] += part
            else:
                out_ref[...] = (total[...] + part).astype(out_ref.dtype)

    if role is None:
        work()
    else:
        pl.when(decoder if role == "decoder" else jnp.logical_not(decoder))(work)


def block(row_choices, queue_choices, weights, name, role=None, after=None):
    gain, merging, upper, lower = weights
    row_count, width = row_choices[0][1].shape
    hidden = upper.shape[1]
    step, merge_step = 1024, 512
    anywhere = pl.BlockSpec(memory_space=pl.ANY)
    resident = pl.BlockSpec(memory_space=pltpu.VMEM)
    after = row_choices[0][1] if after is None else after
    arrays = [array for _, array in row_choices] + [array for _, array in queue_choices]
    return pl.pallas_call(
        functools.partial(
            block_kernel,
            row_sources=[test for test, _ in row_choices],
            queue_sources=[test for test, _ in queue_choices],
            role=role, step=step, merge_step=merge_step,
        ),
        out_shape=jax.ShapeDtypeStruct((row_count, width), jnp.bfloat16),
        in_specs=[anywhere] * len(arrays) + [resident, anywhere, anywhere, anywhere, anywhere],
        out_specs=resident,
        scratch_shapes=[
            pltpu.VMEM((row_count, width), jnp.bfloat16),
            pltpu.VMEM((row_count, width), jnp.bfloat16),
            pltpu.VMEM(merging.shape, jnp.bfloat16),
            pltpu.VMEM(upper.shape, jnp.bfloat16),
            pltpu.VMEM(lower.shape, jnp.bfloat16),
            pltpu.VMEM((row_count, width), jnp.float32),
            pltpu.VMEM((row_count, width), jnp.float32),
            pltpu.SemaphoreType.DMA((2,)),
            pltpu.SemaphoreType.DMA((2 * len(even_spans(width, merge_step)),)),
            pltpu.SemaphoreType.DMA((len(spans(hidden, step)),)),
            pltpu.SemaphoreType.DMA((len(spans(hidden, step)),)),
        ],
        compiler_params=pltpu.CompilerParams(vmem_limit_bytes=48 * 1024 * 1024),
        cost_estimate=pl.CostEstimate(
            flops=2 * row_count * width * (2 * width + 2 * hidden),
            bytes_accessed=2 * (merging.size + upper.size + lower.size + 3 * row_count * width),
            transcendentals=row_count * hidden,
        ),
        name=name,
    )(*arrays, gain, merging, upper, lower, after)


def local(latent_rows, skip_queue, norm_gain, skip_weight, up_weight, down_weight):
    count = lax.axis_size("section")
    half = count // 2
    quarter = half // 2
    section = lax.axis_index("section")
    weights = (norm_gain, skip_weight[0], up_weight[0], down_weight[0])
    step_on = [(source, (source + 1) % count) for source in range(count)]
    handed = [(source, source + quarter) for source in range(quarter)]
    direct = [(source, count - 1 - source) for source in range(quarter, half)]
    passed = [(source + quarter, count - 1 - source) for source in range(quarter)]
    is_near = lambda section: section < half + quarter
    is_far = lambda section: section >= half + quarter

    arrived = move(skip_queue[0], handed + direct)
    output = block([(None, latent_rows[0])], [(None, skip_queue[0])], weights, "tick_0")
    for number in range(1, TICKS):
        rows = move(output, step_on)
        arriving = move(output, handed + direct)
        queue = [(is_near, arrived), (is_far, move(arrived, passed))]
        output = block([(None, rows)], queue, weights, "tick_%d" % number)
        arrived = arriving
    rows = move(output, step_on)
    far = move(arrived, passed)
    queue_now = jnp.where(section >= half, jnp.where(is_far(section), far, arrived), output)
    return (rows[None], queue_now[None])


def solution(mesh):
    return jax.shard_map(
        local,
        mesh=mesh,
        in_specs=(
            P(("groups", "section"), None, None),
            P(("groups", "section"), None, None),
            P("section", None),
            P("section", None, None),
            P("section", None, None),
            P("section", None, None),
        ),
        out_specs=(P(("groups", "section"), None, None), P(("groups", "section"), None, None)),
        check_vma=False,
    )
```

```python
import functools

import jax
import jax.numpy as jnp
from jax import lax
from jax.experimental import pallas as pl
from jax.experimental.pallas import tpu as pltpu
from jax.sharding import PartitionSpec as P

TICKS = 3


epsilon = 1e-06


def move(value, pairs, label):
    with jax.named_scope(label):
        return lax.ppermute(value, "section", pairs)


def spans(extent, step):
    return [(start, min(step, extent - start)) for start in range(0, extent, step)]


def start_one(copies, tests):
    section = lax.axis_index("section")
    for copy, test in zip(copies, tests):
        if test is None:
            copy.start()
        else:
            pl.when(test(section))(copy.start)


def row_pieces(source, target, sems, pieces):
    return [
        pltpu.make_async_copy(source.at[pl.ds(start, size), :], target.at[pl.ds(start, size), :], sems.at[i])
        for i, (start, size) in enumerate(pieces)
    ]


def column_pieces(source, target, sems, pieces):
    return [
        pltpu.make_async_copy(source.at[:, pl.ds(start, size)], target.at[:, pl.ds(start, size)], sems.at[i])
        for i, (start, size) in enumerate(pieces)
    ]


def dot(left, right):
    return jnp.dot(left, right, preferred_element_type=jnp.float32)


def block_kernel(*refs, tests, merge_pieces, pieces, fill):
    queues_hbm, refs = refs[: len(tests)], refs[len(tests) :]
    rows, gain, merging, upper, lower, out = refs[:6]
    rows_copies, merging_copies, upper_copies, lower_copies = [], [], [], []
    if fill:
        merging_hbm, upper_hbm, lower_hbm = merging, upper, lower
        rows_hbm, gain_hbm = rows, gain
        merging, upper, lower, queue, merged, total, queue_sem, rows, gain, rows_sem, merging_sem, upper_sem, lower_sem = refs[6:]
        rows_copies = [
            pltpu.make_async_copy(rows_hbm, rows, rows_sem.at[0]), pltpu.make_async_copy(gain_hbm, gain, rows_sem.at[1])
        ]
        merging_copies = row_pieces(merging_hbm, merging, merging_sem, merge_pieces)
        upper_copies = column_pieces(upper_hbm, upper, upper_sem, pieces)
        lower_copies = row_pieces(lower_hbm, lower, lower_sem, pieces)
    else:
        queue, merged, total, queue_sem = refs[6:]
    decoder = lax.axis_index("section") >= lax.axis_size("section") // 2
    width = rows.shape[1]
    queue_copies = [pltpu.make_async_copy(source, queue, queue_sem.at[0]) for source in queues_hbm]

    feed_copies = [copy for pair in zip(upper_copies, lower_copies) for copy in pair]
    window = 3

    def arrive(copies, number):
        if fill:
            copies[number].wait()
            if number + window < len(copies):
                copies[number + window].start()

    for copy in rows_copies:
        copy.start()

    @pl.when(decoder)
    def _():
        start_one(queue_copies, tests)
        for copy in (merging_copies + feed_copies)[:window]:
            copy.start()

    @pl.when(jnp.logical_not(decoder))
    def _():
        for copy in feed_copies[:window]:
            copy.start()

    for copy in rows_copies:
        copy.wait()

    @pl.when(decoder)
    def _():
        value = None
        for i, (start, size) in enumerate(merge_pieces):
            if start == width:
                queue_copies[0].wait()
            arrive(merging_copies + feed_copies[:window], i)
            source = rows if start < width else queue
            part = dot(source[:, pl.ds(start % width, size)], merging[pl.ds(start, size), :])
            value = part if value is None else value + part
        merged[...] = value

    @pl.when(jnp.logical_not(decoder))
    def _():
        merged[...] = rows[...].astype(jnp.float32)

    value = merged[...]
    center = jnp.mean(value, axis=1, keepdims=True)
    spread = jnp.mean(jnp.square(value - center), axis=1, keepdims=True)
    normed = ((value - center) * lax.rsqrt(spread + epsilon) * gain[...]).astype(jnp.bfloat16)
    for i, (start, size) in enumerate(pieces):
        arrive(feed_copies, 2 * i)
        raised = dot(normed, upper[:, pl.ds(start, size)])
        hidden = jax.nn.gelu(raised, approximate=True).astype(jnp.bfloat16)
        arrive(feed_copies, 2 * i + 1)
        part = dot(hidden, lower[pl.ds(start, size), :])
        if i == 0:
            total[...] = merged[...] + part
        elif i < len(pieces) - 1:
            total[...] += part
        else:
            out[...] = (total[...] + part).astype(out.dtype)


def block(rows, queue_choices, weights, name, fill=False):
    gain, merging, upper, lower = weights
    row_count, width = rows.shape
    hidden = upper.shape[1]
    merge_step = 512 if fill else width
    step = 1024
    merge_pieces = [(base + start, size) for base in (0, width) for start, size in spans(width, merge_step)]
    pieces = spans(hidden, step)
    anywhere = pl.BlockSpec(memory_space=pl.ANY)
    resident = pl.BlockSpec(memory_space=pltpu.VMEM)
    far = pl.BlockSpec(memory_space=pltpu.HBM)
    if fill:
        queue_choices = [(test, pltpu.with_memory_space_constraint(array, pltpu.HBM)) for test, array in queue_choices]
        rows, gain, merging, upper, lower = (
            pltpu.with_memory_space_constraint(array, pltpu.HBM) for array in (rows, gain, merging, upper, lower)
        )
    output = jax.ShapeDtypeStruct((row_count, width), jnp.bfloat16)
    copied = [jax.ShapeDtypeStruct(array.shape, array.dtype) for array in (merging, upper, lower)]
    scratch = [
        pltpu.VMEM((row_count, width), jnp.bfloat16),
        pltpu.VMEM((row_count, width), jnp.float32),
        pltpu.VMEM((row_count, width), jnp.float32),
        pltpu.SemaphoreType.DMA((1,)),
    ]
    if fill:
        scratch += [pltpu.VMEM(rows.shape, rows.dtype), pltpu.VMEM(gain.shape, gain.dtype)]
        scratch += [pltpu.SemaphoreType.DMA((len(some),)) for some in ((rows, gain), merge_pieces, pieces, pieces)]
    return pl.pallas_call(
        functools.partial(
            block_kernel, tests=[test for test, _ in queue_choices], merge_pieces=merge_pieces, pieces=pieces, fill=fill
        ),
        out_shape=[output, *copied] if fill else output,
        in_specs=[anywhere] * len(queue_choices) + [far if fill else resident] * 5,
        out_specs=[resident] * 4 if fill else resident,
        scratch_shapes=scratch,
        compiler_params=pltpu.CompilerParams(vmem_limit_bytes=(16 if fill else 12) * 1024 * 1024),
        cost_estimate=pl.CostEstimate(
            flops=2 * row_count * width * (2 * width + 2 * hidden),
            bytes_accessed=2 * (2 * width * width + 2 * width * hidden + 3 * row_count * width),
            transcendentals=row_count * hidden,
        ),
        name=name,
    )(*(array for _, array in queue_choices), rows, gain, merging, upper, lower)


def local(latent_rows, skip_queue, norm_gain, skip_weight, up_weight, down_weight):
    count = lax.axis_size("section")
    half = count // 2
    quarter = half // 2
    section = lax.axis_index("section")
    weights = (norm_gain, skip_weight[0], up_weight[0], down_weight[0])
    step_on = [(source, (source + 1) % count) for source in range(count)]
    by_hand = [quarter + source for source in range(quarter - 2)] + [half - 1, half - 2]
    handed = list(zip(range(quarter), by_hand))
    direct = [(source, count - 1 - source) for source in range(quarter, half)]
    passed = [(hand, count - 1 - source) for source, hand in handed]
    is_near = lambda section: section < half + quarter
    is_far = lambda section: section >= half + quarter

    late, shifted = 0, quarter - 2
    handed_first = [pair for pair in handed if pair[0] not in (late, shifted)] + [(shifted, quarter)]
    passed_first = [(hand, count - 1 - source) for source, hand in handed_first]
    handed_late = [(late, quarter)]
    passed_late = [(quarter, count - 1 - late)]
    is_late = lambda section: section == count - 1 - late
    is_far_else = lambda section: jnp.logical_and(is_far(section), jnp.logical_not(is_late(section)))

    arrived = move(skip_queue[0], handed + direct, "skip_0_near")
    output, *held = block(latent_rows[0], [(None, skip_queue[0])], weights, "tick_0", fill=True)
    weights = (norm_gain, *held)
    rows = move(output, step_on, "rows_0")
    output, arrived = lax.optimization_barrier((output, arrived))
    passed_0 = move(arrived, passed, "skip_0_far")
    arriving = move(output, handed_first + direct, "skip_1_near")
    arriving_late = move(output, handed_late, "skip_1_late")

    output = block(rows, [(is_near, arrived), (is_far, passed_0)], weights, "tick_1")
    passed_1 = move(arriving, passed_first, "skip_1_far")
    late_1 = move(arriving_late, passed_late, "skip_1_last")
    queue = [(is_near, arriving), (is_far_else, passed_1), (is_late, late_1)]
    rows = move(output, step_on, "rows_1")
    arrived = move(output, handed + direct, "skip_2_near")

    output = block(rows, queue, weights, "tick_2")
    rows = move(output, step_on, "rows_2")
    far = move(arrived, passed, "skip_2_far")
    queue_now = jnp.where(section >= half, jnp.where(is_far(section), far, arrived), output)
    return (rows[None], queue_now[None])


def solution(mesh):
    return jax.shard_map(
        local,
        mesh=mesh,
        in_specs=(
            P(("groups", "section"), None, None),
            P(("groups", "section"), None, None),
            P("section", None),
            P("section", None, None),
            P("section", None, None),
            P("section", None, None),
        ),
        out_specs=(P(("groups", "section"), None, None), P(("groups", "section"), None, None)),
        check_vma=False,
    )
```

```python
import functools

import jax
import jax.numpy as jnp
from jax import lax
from jax.experimental import pallas as pl
from jax.experimental.pallas import tpu as pltpu
from jax.sharding import PartitionSpec as P

TICKS = 3


epsilon = 1e-06


def move(value, pairs, label):
    with jax.named_scope(label):
        return lax.ppermute(value, "section", pairs)


def spans(extent, step):
    return [(start, min(step, extent - start)) for start in range(0, extent, step)]


def start_one(choices, tests):
    section = lax.axis_index("section")

    def start(copies):
        for copy in copies:
            copy.start()

    for copies, (test, _) in zip(choices, tests):
        if test is None:
            start(copies)
        else:
            pl.when(test(section))(functools.partial(start, copies))


def row_pieces(source, target, sems, pieces):
    return [
        pltpu.make_async_copy(source.at[pl.ds(start, size), :], target.at[pl.ds(start, size), :], sems.at[i])
        for i, (start, size) in enumerate(pieces)
    ]


def column_pieces(source, target, sems, pieces):
    return [
        pltpu.make_async_copy(source.at[:, pl.ds(start, size)], target.at[:, pl.ds(start, size)], sems.at[i])
        for i, (start, size) in enumerate(pieces)
    ]


def dot(left, right):
    return jnp.dot(left, right, preferred_element_type=jnp.float32)


def block_kernel(*refs, tests, merge_pieces, pieces, fill):
    count = sum(number for _, number in tests)
    queues_hbm, refs = refs[:count], refs[count:]
    rows, gain, merging, upper, lower, out = refs[:6]
    rows_copies, merging_copies, upper_copies, lower_copies = [], [], [], []
    if fill:
        merging_hbm, upper_hbm, lower_hbm = merging, upper, lower
        rows_hbm, gain_hbm = rows, gain
        merging, upper, lower, queue, merged, total, queue_sem, rows, gain, rows_sem, merging_sem, upper_sem, lower_sem = refs[6:]
        rows_copies = [
            pltpu.make_async_copy(rows_hbm, rows, rows_sem.at[0]), pltpu.make_async_copy(gain_hbm, gain, rows_sem.at[1])
        ]
        merging_copies = row_pieces(merging_hbm, merging, merging_sem, merge_pieces)
        upper_copies = column_pieces(upper_hbm, upper, upper_sem, pieces)
        lower_copies = row_pieces(lower_hbm, lower, lower_sem, pieces)
    else:
        queue, merged, total, queue_sem = refs[6:]
    decoder = lax.axis_index("section") >= lax.axis_size("section") // 2
    width = rows.shape[1]
    top = queue.shape[0] // 2
    halves = [(0, top), (top, queue.shape[0] - top)]
    queue_copies = []
    for test, number in tests:
        sources, queues_hbm = queues_hbm[:number], queues_hbm[number:]
        parts = [sources[0].at[pl.ds(start, size), :] for start, size in halves] if number == 1 else sources
        queue_copies.append(
            [
                pltpu.make_async_copy(part, queue.at[pl.ds(start, size), :], queue_sem.at[i])
                for i, (part, (start, size)) in enumerate(zip(parts, halves))
            ]
        )

    feed_copies = [copy for pair in zip(upper_copies, lower_copies) for copy in pair]
    window = 3

    def arrive(copies, number):
        if fill:
            copies[number].wait()
            if number + window < len(copies):
                copies[number + window].start()

    for copy in rows_copies:
        copy.start()

    @pl.when(decoder)
    def _():
        start_one(queue_copies, tests)
        for copy in (merging_copies + feed_copies)[:window]:
            copy.start()

    @pl.when(jnp.logical_not(decoder))
    def _():
        for copy in feed_copies[:window]:
            copy.start()

    for copy in rows_copies:
        copy.wait()

    @pl.when(decoder)
    def _():
        value = None
        for i, (start, size) in enumerate(merge_pieces):
            if start == width:
                for copy in queue_copies[0]:
                    copy.wait()
            arrive(merging_copies + feed_copies[:window], i)
            source = rows if start < width else queue
            part = dot(source[:, pl.ds(start % width, size)], merging[pl.ds(start, size), :])
            value = part if value is None else value + part
        merged[...] = value

    @pl.when(jnp.logical_not(decoder))
    def _():
        merged[...] = rows[...].astype(jnp.float32)

    value = merged[...]
    center = jnp.mean(value, axis=1, keepdims=True)
    spread = jnp.mean(jnp.square(value - center), axis=1, keepdims=True)
    normed = ((value - center) * lax.rsqrt(spread + epsilon) * gain[...]).astype(jnp.bfloat16)
    for i, (start, size) in enumerate(pieces):
        arrive(feed_copies, 2 * i)
        raised = dot(normed, upper[:, pl.ds(start, size)])
        hidden = jax.nn.gelu(raised, approximate=True).astype(jnp.bfloat16)
        arrive(feed_copies, 2 * i + 1)
        part = dot(hidden, lower[pl.ds(start, size), :])
        if i == 0:
            total[...] = merged[...] + part
        elif i < len(pieces) - 1:
            total[...] += part
        else:
            out[...] = (total[...] + part).astype(out.dtype)


def block(rows, queue_choices, weights, name, fill=False):
    gain, merging, upper, lower = weights
    queue_choices = [(test, arrays if isinstance(arrays, list) else [arrays]) for test, arrays in queue_choices]
    operand_count = sum(len(arrays) for _, arrays in queue_choices)
    row_count, width = rows.shape
    hidden = upper.shape[1]
    merge_step = 512 if fill else width
    step = 1024
    merge_pieces = [(base + start, size) for base in (0, width) for start, size in spans(width, merge_step)]
    pieces = spans(hidden, step)
    anywhere = pl.BlockSpec(memory_space=pl.ANY)
    resident = pl.BlockSpec(memory_space=pltpu.VMEM)
    far = pl.BlockSpec(memory_space=pltpu.HBM)
    if fill:
        queue_choices = [
            (test, [pltpu.with_memory_space_constraint(array, pltpu.HBM) for array in arrays])
            for test, arrays in queue_choices
        ]
        rows, gain, merging, upper, lower = (
            pltpu.with_memory_space_constraint(array, pltpu.HBM) for array in (rows, gain, merging, upper, lower)
        )
    output = jax.ShapeDtypeStruct((row_count, width), jnp.bfloat16)
    copied = [jax.ShapeDtypeStruct(array.shape, array.dtype) for array in (merging, upper, lower)]
    scratch = [
        pltpu.VMEM((row_count, width), jnp.bfloat16),
        pltpu.VMEM((row_count, width), jnp.float32),
        pltpu.VMEM((row_count, width), jnp.float32),
        pltpu.SemaphoreType.DMA((2,)),
    ]
    if fill:
        scratch += [pltpu.VMEM(rows.shape, rows.dtype), pltpu.VMEM(gain.shape, gain.dtype)]
        scratch += [pltpu.SemaphoreType.DMA((len(some),)) for some in ((rows, gain), merge_pieces, pieces, pieces)]
    return pl.pallas_call(
        functools.partial(
            block_kernel, tests=[(test, len(arrays)) for test, arrays in queue_choices], merge_pieces=merge_pieces, pieces=pieces, fill=fill
        ),
        out_shape=[output, *copied] if fill else output,
        in_specs=[anywhere] * operand_count + [far if fill else resident] * 5,
        out_specs=[resident] * 4 if fill else resident,
        scratch_shapes=scratch,
        compiler_params=pltpu.CompilerParams(vmem_limit_bytes=(16 if fill else 12) * 1024 * 1024),
        cost_estimate=pl.CostEstimate(
            flops=2 * row_count * width * (2 * width + 2 * hidden),
            bytes_accessed=2 * (2 * width * width + 2 * width * hidden + 3 * row_count * width),
            transcendentals=row_count * hidden,
        ),
        name=name,
    )(*(array for _, arrays in queue_choices for array in arrays), rows, gain, merging, upper, lower)


def local(latent_rows, skip_queue, norm_gain, skip_weight, up_weight, down_weight):
    count = lax.axis_size("section")
    half = count // 2
    quarter = half // 2
    section = lax.axis_index("section")
    weights = (norm_gain, skip_weight[0], up_weight[0], down_weight[0])
    step_on = [(source, (source + 1) % count) for source in range(count)]
    handed = [(source, half - 1 - source) for source in range(quarter)]
    direct = [(source, count - 1 - source) for source in range(quarter, half)]
    passed = [(hand, count - 1 - source) for source, hand in handed]
    is_near = lambda section: section < half + quarter
    is_far = lambda section: section >= half + quarter
    split = [(0, (quarter, quarter + 1)), (1, (half - 2, half - 1))]
    handed_half = [[(source, hands[part]) for source, hands in split] for part in (0, 1)]
    passed_half = [[(hands[part], count - 1 - source) for source, hands in split] for part in (0, 1)]
    is_split = lambda section: section >= count - len(split)
    is_whole = lambda section: jnp.logical_and(is_far(section), jnp.logical_not(is_split(section)))

    arrived = move(skip_queue[0], handed + direct, "skip_0_near")
    output, *held = block(latent_rows[0], [(None, skip_queue[0])], weights, "tick_0", fill=True)
    weights = (norm_gain, *held)
    rows = move(output, step_on, "rows_0")
    output, arrived = lax.optimization_barrier((output, arrived))
    passed_0 = move(arrived, passed, "skip_0_far")
    arriving = move(output, handed[len(split) :] + direct, "skip_1_near")
    top = output.shape[0] // 2
    halves = [move(part, pairs, "skip_1_halves") for part, pairs in zip((output[:top], output[top:]), handed_half)]

    output = block(rows, [(is_near, arrived), (is_far, passed_0)], weights, "tick_1")
    passed_1 = move(arriving, passed[len(split) :], "skip_1_far")
    halves = [move(part, pairs, "skip_1_far_halves") for part, pairs in zip(halves, passed_half)]
    queue = [(is_near, arriving), (is_whole, passed_1), (is_split, halves)]
    rows = move(output, step_on, "rows_1")
    arrived = move(output, handed + direct, "skip_2_near")

    output = block(rows, queue, weights, "tick_2")
    rows = move(output, step_on, "rows_2")
    far = move(arrived, passed, "skip_2_far")
    queue_now = jnp.where(section >= half, jnp.where(is_far(section), far, arrived), output)
    return (rows[None], queue_now[None])


def solution(mesh):
    return jax.shard_map(
        local,
        mesh=mesh,
        in_specs=(
            P(("groups", "section"), None, None),
            P(("groups", "section"), None, None),
            P("section", None),
            P("section", None, None),
            P("section", None, None),
            P("section", None, None),
        ),
        out_specs=(P(("groups", "section"), None, None), P(("groups", "section"), None, None)),
        check_vma=False,
    )
```

```python
import functools

import jax
import jax.numpy as jnp
from jax import lax
from jax.experimental import pallas as pl
from jax.experimental.pallas import tpu as pltpu
from jax.sharding import PartitionSpec as P

TICKS = 3


epsilon = 1e-06
CUT = 4


def move(value, pairs, label):
    with jax.named_scope(label):
        return lax.ppermute(value, "section", pairs)


def spans(extent, step):
    return [(start, min(step, extent - start)) for start in range(0, extent, step)]


def start_one(choices, tests):
    section = lax.axis_index("section")

    def start(copies):
        for copy in copies:
            copy.start()

    for copies, (test, _) in zip(choices, tests):
        if test is None:
            start(copies)
        else:
            pl.when(test(section))(functools.partial(start, copies))


def row_pieces(source, target, sems, pieces):
    return [
        pltpu.make_async_copy(source.at[pl.ds(start, size), :], target.at[pl.ds(start, size), :], sems.at[i])
        for i, (start, size) in enumerate(pieces)
    ]


def column_pieces(source, target, sems, pieces):
    return [
        pltpu.make_async_copy(source.at[:, pl.ds(start, size)], target.at[:, pl.ds(start, size)], sems.at[i])
        for i, (start, size) in enumerate(pieces)
    ]


def dot(left, right):
    return jnp.dot(left, right, preferred_element_type=jnp.float32)


def block_kernel(*refs, tests, merge_pieces, pieces, fill):
    count = sum(number for _, number in tests)
    queues_hbm, refs = refs[:count], refs[count:]
    rows, gain, merging, upper, lower, out = refs[:6]
    rows_copies, merging_copies, upper_copies, lower_copies = [], [], [], []
    if fill:
        merging_hbm, upper_hbm, lower_hbm = merging, upper, lower
        rows_hbm, gain_hbm = rows, gain
        merging, upper, lower, queue, merged, total, queue_sem, rows, gain, rows_sem, merging_sem, upper_sem, lower_sem = refs[6:]
        rows_copies = [
            pltpu.make_async_copy(rows_hbm, rows, rows_sem.at[0]), pltpu.make_async_copy(gain_hbm, gain, rows_sem.at[1])
        ]
        merging_copies = row_pieces(merging_hbm, merging, merging_sem, merge_pieces)
        upper_copies = column_pieces(upper_hbm, upper, upper_sem, pieces)
        lower_copies = row_pieces(lower_hbm, lower, lower_sem, pieces)
    else:
        queue, merged, total, queue_sem = refs[6:]
    decoder = lax.axis_index("section") >= lax.axis_size("section") // 2
    width = rows.shape[1]
    cut = queue.shape[0] // CUT
    pieces_of = [(0, cut), (cut, queue.shape[0] - cut)]
    queue_copies = []
    for test, number in tests:
        sources, queues_hbm = queues_hbm[:number], queues_hbm[number:]
        parts = [sources[0].at[pl.ds(start, size), :] for start, size in pieces_of] if number == 1 else sources
        queue_copies.append(
            [
                pltpu.make_async_copy(part, queue.at[pl.ds(start, size), :], queue_sem.at[i])
                for i, (part, (start, size)) in enumerate(zip(parts, pieces_of))
            ]
        )

    feed_copies = [copy for pair in zip(upper_copies, lower_copies) for copy in pair]
    window = 3

    def arrive(copies, number):
        if fill:
            copies[number].wait()
            if number + window < len(copies):
                copies[number + window].start()

    for copy in rows_copies:
        copy.start()

    @pl.when(decoder)
    def _():
        start_one(queue_copies, tests)
        for copy in (merging_copies + feed_copies)[:window]:
            copy.start()

    @pl.when(jnp.logical_not(decoder))
    def _():
        for copy in feed_copies[:window]:
            copy.start()

    for copy in rows_copies:
        copy.wait()

    @pl.when(decoder)
    def _():
        value = None
        for i, (start, size) in enumerate(merge_pieces):
            if start == width:
                for copy in queue_copies[0]:
                    copy.wait()
            arrive(merging_copies + feed_copies[:window], i)
            source = rows if start < width else queue
            part = dot(source[:, pl.ds(start % width, size)], merging[pl.ds(start, size), :])
            value = part if value is None else value + part
        merged[...] = value

    @pl.when(jnp.logical_not(decoder))
    def _():
        merged[...] = rows[...].astype(jnp.float32)

    value = merged[...]
    center = jnp.mean(value, axis=1, keepdims=True)
    spread = jnp.mean(jnp.square(value - center), axis=1, keepdims=True)
    normed = ((value - center) * lax.rsqrt(spread + epsilon) * gain[...]).astype(jnp.bfloat16)
    for i, (start, size) in enumerate(pieces):
        arrive(feed_copies, 2 * i)
        raised = dot(normed, upper[:, pl.ds(start, size)])
        hidden = jax.nn.gelu(raised, approximate=True).astype(jnp.bfloat16)
        arrive(feed_copies, 2 * i + 1)
        part = dot(hidden, lower[pl.ds(start, size), :])
        if i == 0:
            total[...] = merged[...] + part
        elif i < len(pieces) - 1:
            total[...] += part
        else:
            out[...] = (total[...] + part).astype(out.dtype)


def block(rows, queue_choices, weights, name, fill=False):
    gain, merging, upper, lower = weights
    queue_choices = [(test, arrays if isinstance(arrays, list) else [arrays]) for test, arrays in queue_choices]
    operand_count = sum(len(arrays) for _, arrays in queue_choices)
    row_count, width = rows.shape
    hidden = upper.shape[1]
    merge_step = 512 if fill else width
    step = 1024
    merge_pieces = [(base + start, size) for base in (0, width) for start, size in spans(width, merge_step)]
    pieces = spans(hidden, step)
    anywhere = pl.BlockSpec(memory_space=pl.ANY)
    resident = pl.BlockSpec(memory_space=pltpu.VMEM)
    far = pl.BlockSpec(memory_space=pltpu.HBM)
    if fill:
        queue_choices = [
            (test, [pltpu.with_memory_space_constraint(array, pltpu.HBM) for array in arrays])
            for test, arrays in queue_choices
        ]
        rows, gain, merging, upper, lower = (
            pltpu.with_memory_space_constraint(array, pltpu.HBM) for array in (rows, gain, merging, upper, lower)
        )
    output = jax.ShapeDtypeStruct((row_count, width), jnp.bfloat16)
    copied = [jax.ShapeDtypeStruct(array.shape, array.dtype) for array in (merging, upper, lower)]
    scratch = [
        pltpu.VMEM((row_count, width), jnp.bfloat16),
        pltpu.VMEM((row_count, width), jnp.float32),
        pltpu.VMEM((row_count, width), jnp.float32),
        pltpu.SemaphoreType.DMA((2,)),
    ]
    if fill:
        scratch += [pltpu.VMEM(rows.shape, rows.dtype), pltpu.VMEM(gain.shape, gain.dtype)]
        scratch += [pltpu.SemaphoreType.DMA((len(some),)) for some in ((rows, gain), merge_pieces, pieces, pieces)]
    return pl.pallas_call(
        functools.partial(
            block_kernel, tests=[(test, len(arrays)) for test, arrays in queue_choices], merge_pieces=merge_pieces, pieces=pieces, fill=fill
        ),
        out_shape=[output, *copied] if fill else output,
        in_specs=[anywhere] * operand_count + [far if fill else resident] * 5,
        out_specs=[resident] * 4 if fill else resident,
        scratch_shapes=scratch,
        compiler_params=pltpu.CompilerParams(vmem_limit_bytes=(16 if fill else 12) * 1024 * 1024),
        cost_estimate=pl.CostEstimate(
            flops=2 * row_count * width * (2 * width + 2 * hidden),
            bytes_accessed=2 * (2 * width * width + 2 * width * hidden + 3 * row_count * width),
            transcendentals=row_count * hidden,
        ),
        name=name,
    )(*(array for _, arrays in queue_choices for array in arrays), rows, gain, merging, upper, lower)


def place_kernel(*refs, tests):
    sources, out, sem = refs[: len(tests)], refs[-2], refs[-1]
    copies = [pltpu.make_async_copy(source, out.at[0], sem.at[0]) for source in sources]
    start_one([[copy] for copy in copies], [(test, 1) for test in tests])
    copies[0].wait()


def place(choices, name, after=()):
    shape, dtype = choices[0][1].shape, choices[0][1].dtype
    anywhere = pl.BlockSpec(memory_space=pl.ANY)
    return pl.pallas_call(
        functools.partial(place_kernel, tests=[test for test, _ in choices]),
        out_shape=jax.ShapeDtypeStruct((1, *shape), dtype),
        in_specs=[pl.BlockSpec(memory_space=pltpu.VMEM)] * len(choices) + [anywhere] * len(after),
        out_specs=anywhere,
        scratch_shapes=[pltpu.SemaphoreType.DMA((1,))],
        compiler_params=pltpu.CompilerParams(vmem_limit_bytes=1024 * 1024),
        name=name,
    )(*(array for _, array in choices), *(pltpu.with_memory_space_constraint(array, pltpu.HBM) for array in after))


def local(latent_rows, skip_queue, norm_gain, skip_weight, up_weight, down_weight):
    count = lax.axis_size("section")
    half = count // 2
    quarter = half // 2
    section = lax.axis_index("section")
    weights = (norm_gain, skip_weight[0], up_weight[0], down_weight[0])
    step_on = [(source, (source + 1) % count) for source in range(count)]
    handed = [(source, half - 1 - source) for source in range(quarter)]
    direct = [(source, count - 1 - source) for source in range(quarter, half)]
    passed = [(hand, count - 1 - source) for source, hand in handed]
    is_near = lambda section: section < half + quarter
    is_far = lambda section: section >= half + quarter
    split = [(0, (quarter, quarter + 1)), (1, (quarter + 1, half - 2))]
    handed_piece = [[(source, hands[part]) for source, hands in split] for part in (0, 1)]
    passed_piece = [[(hands[part], count - 1 - source) for source, hands in split] for part in (0, 1)]
    is_split = lambda section: section >= count - len(split)
    is_whole = lambda section: jnp.logical_and(is_far(section), jnp.logical_not(is_split(section)))
    top = latent_rows.shape[1] // CUT

    skip = skip_queue[0]
    near = move(skip, handed + direct, "skip_0_near")
    output, *held = block(latent_rows[0], [(None, skip)], weights, "tick_0", fill=True)
    weights = (norm_gain, *held)
    rows = move(output, step_on, "rows_0")
    output, near = lax.optimization_barrier((output, near))
    queue = [(is_near, near), (is_far, move(near, passed, "skip_0_far"))]
    near = move(output, direct, "skip_1_near")
    hand = move(output, handed[len(split) :], "skip_1_handed")
    pieces = [move(part, pairs, "skip_1_pieces") for part, pairs in zip((output[:top], output[top:]), handed_piece)]

    output = block(rows, queue, weights, "tick_1")
    far = move(hand, passed[len(split) :], "skip_1_far")
    pieces = [move(part, pairs, "skip_1_far_pieces") for part, pairs in zip(pieces, passed_piece)]
    queue = [(is_near, near), (is_whole, far), (is_split, pieces)]
    rows = move(output, step_on, "rows_1")
    near = move(output, handed + direct, "skip_2_near")

    output = block(rows, queue, weights, "tick_2")
    rows = move(output, step_on, "rows_2")
    far = move(near, passed, "skip_2_far")
    is_encoder = lambda section: section < half
    is_near_decoder = lambda section: jnp.logical_and(section >= half, is_near(section))
    next_rows = place([(None, rows)], "place_rows")
    choices = [(is_encoder, output), (is_near_decoder, near), (is_far, far)]
    next_queue = place(choices, "place_queue", after=(next_rows,))
    return (next_rows, next_queue)


def solution(mesh):
    return jax.shard_map(
        local,
        mesh=mesh,
        in_specs=(
            P(("groups", "section"), None, None),
            P(("groups", "section"), None, None),
            P("section", None),
            P("section", None, None),
            P("section", None, None),
            P("section", None, None),
        ),
        out_specs=(P(("groups", "section"), None, None), P(("groups", "section"), None, None)),
        check_vma=False,
    )
```
